32 devices in a mesh: ctx: 8 (over y, x, core), exp: 4 (over z).
Axes of the slice: x: 2, y: 2, z: 4, core: 2. Of those that a mesh axis runs over, the one named last changes fastest.
Arguments:
- hidden: bfloat16 [4096, 2048], P(('ctx', 'exp')), may hold values from -6 to 6
- queries: bfloat16 [4096, 2048], P(('ctx', 'exp')), may hold values from -16 to 16
- keys: bfloat16 [4096, 256], P(('ctx', 'exp')), may hold values from -4 to 4
- values: bfloat16 [4096, 256], P(('ctx', 'exp')), may hold values from -6 to 6
- w_out: bfloat16 [2048, 2048], replicated, may hold values from -0.125 to 0.125
- norm_gain: float32 [2048], replicated, may hold values from 0.5 to 1.5
- w_router: bfloat16 [2048, 128], replicated, may hold values from -0.125 to 0.125
- expert_ids: int32 [4096, 8], P(('ctx', 'exp')), may hold values from 0 to 127, all different within a row; in each aligned block of 128 rows (0 to 127, 128 to 255, ...) at most 9 rows name the same one
- w_gate: bfloat16 [128, 2048, 768], P(('ctx', 'exp')), may hold values from -0.125 to 0.125
- w_up: bfloat16 [128, 2048, 768], P(('ctx', 'exp')), may hold values from -0.125 to 0.125
- w_down: bfloat16 [128, 768, 2048], P(('ctx', 'exp')), may hold values from -0.21875 to 0.21875
Outputs:
- mixed: bfloat16 [4096, 2048], P(('ctx', 'exp'))
The draws below stay inside these ranges and needn't reach their ends.
Inputs may be any that keep to these rules, and one draw needn't show every extreme that they name: `expert_ids`: within the 128 tokens of one device, no expert is named by more than 9 of their routes, a bound that some block reaches of them; a token's experts are distinct.
All inputs are finite; a program needn't handle non-finite values.
Results may differ from the reference program's by a relative error of at most 0.01.
Values may be sent and summed in bfloat16 or wider, within the bound.
A program may use at most 192 MiB of HBM per device.

```python
import math
import jax
import jax.numpy as jnp
import numpy as np
from jax import lax

D = 2048
HQ = 16
HK = 2
DH = 128
E = 128
F = 768
TOP = 8
TOK_DEV = 128
TOKENS = 4096
CAP = 9


def joint_draw(key):
    key_query = jax.random.fold_in(key, 101)
    key_keys = jax.random.fold_in(key, 202)
    keys_f = jnp.clip(jax.random.normal(key_keys, (TOKENS, HK * DH), jnp.float32), -4.0, 4.0)
    query_f = jnp.clip(jax.random.normal(key_query, (TOKENS, HQ * DH), jnp.float32), -4.0, 4.0)
    return (query_f, keys_f)


def draw_queries(key, part):
    return joint_draw(key)[0].astype(jnp.bfloat16)


def draw_keys(key, part):
    return joint_draw(key)[1].astype(jnp.bfloat16)


def block_levels(own_key, shape, cuts, smallest, largest):
    gain = 1.0
    for dim, blocks in cuts:
        heights = jax.random.uniform(jax.random.fold_in(jax.random.fold_in(own_key, 6), dim), (blocks,), jnp.float32, smallest / len(cuts), largest / len(cuts))
        gain = gain * jnp.repeat(jnp.exp(heights), shape[dim] // blocks).reshape((-1,) + (1,) * (len(shape) - 1 - dim))
    return gain


def routed_block(own_key, own, number, rows, amount, top, bound, lean):
    order = jax.random.permutation(own_key, amount)
    crowded, common = portions_of(amount, rows * top, bound, lean, True), portions_of(amount, rows * top, bound, lean, False)
    places = jnp.arange(amount)

    def named(lengths, offset_by):
        used = int((lengths > 0).sum())
        fixed = max(1, used // 4)
        passed = fixed + (places - fixed + offset_by * (used - fixed)) % max(1, amount - fixed)
        return jnp.zeros((amount,), jnp.int32).at[order[jnp.where(places < fixed, places, passed)]].set(jnp.asarray(lengths, jnp.int32))

    lengths = jnp.where(number % 4 == 0, named(crowded, number // 4), named(common, number - number // 4 - 1))
    mixed = jax.random.permutation(jax.random.fold_in(own, 3), amount)
    giver, sink = mixed[0:amount // 2 * 2:2], mixed[1:amount // 2 * 2:2]
    slack = jnp.minimum(lengths[giver] - 1, bound - lengths[sink]) // 2
    slack = jnp.where((giver == order[0]) | (sink == order[0]) | (lengths[sink] == 0), 0, jnp.maximum(slack, 0))
    passed = jax.random.randint(jax.random.fold_in(own, 4), (amount // 2,), 0, 1 << 20) % (slack + 1)
    lengths = lengths.at[giver].add(-passed).at[sink].add(passed)
    labels = jnp.searchsorted(jnp.cumsum(lengths), jnp.arange(rows * top), side="right").astype(jnp.int32)
    grid = labels.reshape(top, rows).T
    grid = grid[jax.random.permutation(jax.random.fold_in(own, 1), rows)]
    offset_by = jax.random.randint(jax.random.fold_in(own, 2), (rows, 1), 0, top)
    return jnp.take_along_axis(grid, (jnp.arange(top)[None, :] + offset_by) % top, axis=1)


def portions_of(count, total, most, lean, full):
    loads = [(1 << 20) // math.isqrt(grade ** lean) + 1 for grade in range(1, count + 1)]
    largest = most if full else min(most, max(-(-total // count), total * loads[0] // sum(loads)))
    least = 1 if total - largest >= count - 1 else 0
    given, spare = [largest] + [least] * (count - 1), total - largest - least * (count - 1)
    while spare > 0:
        free = [i for i in range(1, count) if given[i] < largest] or [i for i in range(1, count) if given[i] < most]
        pool, budget = sum([loads[i] for i in free]), spare
        for i in free:
            extra = min(most - given[i], max(1, budget * loads[i] // pool), spare)
            given[i] = given[i] + extra
            spare = spare - extra
    return np.array(given)


def gaussian(stream_key, shape, deviation, most, pieces=(), kind=jnp.bfloat16):
    entries = deviation * jax.random.normal(stream_key, shape, jnp.float32)
    if pieces:
        entries = entries * block_levels(stream_key, shape, pieces, -0.22, 0.18)
    return jnp.clip(entries, -most, most).astype(kind)


def setup_inputs(seed: int = 0) -> dict:
    streams_of = jax.random.split(jax.random.key(seed), 12)
    hidden = gaussian(streams_of[0], (TOKENS, D), 1.0, 6.0, ((0, 32),))
    queries = draw_queries(jax.random.fold_in(streams_of[11], 71), 0)
    keys = draw_keys(jax.random.fold_in(streams_of[11], 71), 0)
    values = gaussian(streams_of[3], (TOKENS, HK * DH), 1.0, 6.0, ((0, 32),))
    w_out = gaussian(streams_of[4], (HQ * DH, D), (HQ * DH) ** -0.5, 0.125)
    norm_gain = jnp.clip(1.0 + 0.1 * jax.random.normal(streams_of[5], (D,), jnp.float32), 0.5, 1.5)
    w_router = gaussian(streams_of[6], (D, E), D ** -0.5, 0.125)
    expert_ids_keys = jax.random.split(jax.random.fold_in(streams_of[7], 1), TOKENS // TOK_DEV)
    expert_ids_turns = jax.random.permutation(jax.random.fold_in(streams_of[7], 3), TOKENS // TOK_DEV)
    expert_ids = jax.vmap(lambda own, number: routed_block(jax.random.fold_in(streams_of[7], 2), own, number, TOK_DEV, E, TOP, CAP, 2))(expert_ids_keys, expert_ids_turns).reshape((TOKENS, TOP))
    w_gate = gaussian(streams_of[8], (E, D, F), D ** -0.5, 0.125, ((0, 32),))
    w_up = gaussian(streams_of[9], (E, D, F), D ** -0.5, 0.125, ((0, 32),))
    w_down = gaussian(streams_of[10], (E, F, D), F ** -0.5, 0.21875, ((0, 32),))
    return dict(hidden=hidden, queries=queries, keys=keys, values=values, w_out=w_out, norm_gain=norm_gain, w_router=w_router, expert_ids=expert_ids, w_gate=w_gate, w_up=w_up, w_down=w_down)


rope_base = 1000000.0
yarn_factor = 4.0
orig_len = 32768.0
beta_fast = 32.0
beta_slow = 1.0
mscale_yarn = 0.1 * math.log(4.0) + 1.0

def yarn_tables(positions, head_size):
    half_size = head_size // 2
    index_f = jnp.arange(half_size, dtype=jnp.float32)
    pos_freq = rope_base ** (2.0 * index_f / head_size)
    inv_extra = 1.0 / pos_freq
    inv_inter = 1.0 / (yarn_factor * pos_freq)
    low_dim = max(math.floor(head_size * math.log(orig_len / (beta_fast * 2.0 * math.pi)) / (2.0 * math.log(rope_base))), 0)
    high_dim = min(math.ceil(head_size * math.log(orig_len / (beta_slow * 2.0 * math.pi)) / (2.0 * math.log(rope_base))), head_size - 1)
    ramp_part = jnp.clip((index_f - low_dim) / max(high_dim - low_dim, 0.001), 0.0, 1.0)
    extra_part = 1.0 - ramp_part
    inverse = inv_inter * (1.0 - extra_part) + inv_extra * extra_part
    angles = positions.astype(jnp.float32)[:, None] * inverse[None, :]
    angles = jnp.concatenate([angles, angles], axis=-1)
    return (jnp.cos(angles) * mscale_yarn, jnp.sin(angles) * mscale_yarn)

def rotate(vectors, cos_table, sin_table):
    values_f = vectors.astype(jnp.float32)
    half_size = values_f.shape[-1] // 2
    turned = jnp.concatenate([-values_f[..., half_size:], values_f[..., :half_size]], axis=-1)
    return (values_f * cos_table[:, None, :] + turned * sin_table[:, None, :]).astype(jnp.bfloat16)

def reference(hidden, queries, keys, values, w_out, norm_gain, w_router, expert_ids, w_gate, w_up, w_down):
    group = HQ // HK
    block_rows = math.gcd(TOKENS, 256)
    positions = jnp.arange(TOKENS, dtype=jnp.int32)
    cos_table, sin_table = yarn_tables(positions, DH)
    q_rot = rotate(queries.reshape(TOKENS, HQ, DH), cos_table, sin_table)
    q_blocks = q_rot.reshape(TOKENS // block_rows, block_rows, HK, group, DH)
    k_rot = rotate(keys.reshape(TOKENS, HK, DH), cos_table, sin_table).astype(jnp.float32)
    v_all = values.reshape(TOKENS, HK, DH).astype(jnp.float32)
    key_rows = jnp.arange(TOKENS, dtype=jnp.int32)
    block_starts = jnp.arange(TOKENS // block_rows, dtype=jnp.int32) * block_rows
    scale = 1.0 / math.sqrt(DH)

    def attend(operands):
        q_block, q_start = operands
        scores = jnp.einsum('thgd,phd->thgp', q_block.astype(jnp.float32), k_rot) * scale
        q_rows = q_start + jnp.arange(block_rows, dtype=jnp.int32)
        allowed = (key_rows[None, :] <= q_rows[:, None])[:, None, None, :]
        scores = jnp.where(allowed, scores, -1e+30)
        peak = lax.optimization_barrier(jnp.max(scores, axis=-1, keepdims=True))
        weights = jnp.where(allowed, jnp.exp(scores - peak), 0.0)
        total = lax.optimization_barrier(jnp.sum(weights, axis=-1))
        rounded = lax.optimization_barrier(weights.astype(jnp.bfloat16))
        summed = jnp.einsum('thgp,phd->thgd', rounded.astype(jnp.float32), v_all)
        return (summed / total[..., None]).astype(jnp.bfloat16).reshape(block_rows, HQ * DH)
    attn = lax.map(attend, (q_blocks, block_starts)).reshape(TOKENS, HQ * DH)
    h1 = (jnp.dot(attn, w_out, preferred_element_type=jnp.float32) + hidden.astype(jnp.float32)).astype(jnp.bfloat16)
    h1_f = h1.astype(jnp.float32)
    normed = h1_f / jnp.sqrt(lax.optimization_barrier(jnp.mean(h1_f * h1_f, axis=-1, keepdims=True)) + 1e-06) * norm_gain[None, :]
    hn = normed.astype(jnp.bfloat16)
    logits = jnp.dot(hn, w_router, preferred_element_type=jnp.float32)
    chosen = jnp.take_along_axis(logits, expert_ids, axis=1)
    raised = jnp.exp(chosen)
    route_w = (raised / lax.optimization_barrier(jnp.sum(raised, axis=-1, keepdims=True))).astype(jnp.bfloat16)
    num_blocks = TOKENS // TOK_DEV
    onehot = (expert_ids[:, :, None] == jnp.arange(E, dtype=jnp.int32)[None, None, :]).astype(jnp.int32)
    counts = jnp.cumsum(onehot.reshape(num_blocks, TOK_DEV * TOP, E), axis=1).reshape(TOKENS, TOP, E)
    slot = lax.optimization_barrier(jnp.sum(onehot * counts, axis=-1)) - 1
    token_ids = jnp.arange(TOKENS, dtype=jnp.int32)
    buffer_row = ((token_ids // TOK_DEV)[:, None] * CAP + slot).astype(jnp.int32)
    table = jnp.full((E, num_blocks * CAP), TOKENS, dtype=jnp.int32)
    table = table.at[expert_ids, buffer_row].set(jnp.broadcast_to(token_ids[:, None], (TOKENS, TOP)))
    hn_pad = jnp.concatenate([hn, jnp.zeros((1, D), jnp.bfloat16)], axis=0)

    def expert(operands):
        index_rows, gate_e, up_e, down_e = operands
        inputs_rows = hn_pad[index_rows]
        gate_v = jnp.dot(inputs_rows, gate_e, preferred_element_type=jnp.float32)
        up_v = jnp.dot(inputs_rows, up_e, preferred_element_type=jnp.float32)
        active = (jax.nn.silu(gate_v) * up_v).astype(jnp.bfloat16)
        return jnp.dot(active, down_e, preferred_element_type=jnp.float32).astype(jnp.bfloat16)
    outputs = lax.map(expert, (table, w_gate, w_up, w_down))
    total_out = h1_f
    for choice_k in range(TOP):
        picked = outputs[expert_ids[:, choice_k], buffer_row[:, choice_k]].astype(jnp.float32)
        total_out = total_out + route_w[:, choice_k].astype(jnp.float32)[:, None] * picked
    return total_out.astype(jnp.bfloat16)
```

```python
import functools
import math

import jax
import jax.numpy as jnp
import numpy as np
from jax import lax
from jax.experimental import pallas as pl
from jax.experimental.pallas import tpu as pltpu
from jax.sharding import PartitionSpec as P

DH = 128
CAP = 9


rope_base = 1000000.0
yarn_factor = 4.0
orig_len = 32768.0
beta_fast = 32.0
beta_slow = 1.0
mscale_yarn = 0.1 * math.log(4.0) + 1.0


def yarn_tables(positions, head_size):
    half_size = head_size // 2
    index_f = jnp.arange(half_size, dtype=jnp.float32)
    pos_freq = rope_base ** (2.0 * index_f / head_size)
    inv_extra = 1.0 / pos_freq
    inv_inter = 1.0 / (yarn_factor * pos_freq)
    low_dim = max(
        math.floor(
            head_size
            * math.log(orig_len / (beta_fast * 2.0 * math.pi))
            / (2.0 * math.log(rope_base))
        ),
        0,
    )
    high_dim = min(
        math.ceil(
            head_size
            * math.log(orig_len / (beta_slow * 2.0 * math.pi))
            / (2.0 * math.log(rope_base))
        ),
        head_size - 1,
    )
    ramp_part = jnp.clip((index_f - low_dim) / max(high_dim - low_dim, 0.001), 0.0, 1.0)
    extra_part = 1.0 - ramp_part
    inverse = inv_inter * (1.0 - extra_part) + inv_extra * extra_part
    angles = positions.astype(jnp.float32)[:, None] * inverse[None, :]
    angles = jnp.concatenate([angles, angles], axis=-1)
    return (jnp.cos(angles) * mscale_yarn, jnp.sin(angles) * mscale_yarn)


def rotate(vectors, cos_table, sin_table):
    values_f = vectors.astype(jnp.float32)
    half_size = values_f.shape[-1] // 2
    turned = jnp.concatenate([-values_f[..., half_size:], values_f[..., :half_size]], axis=-1)
    return (values_f * cos_table[:, None, :] + turned * sin_table[:, None, :]).astype(jnp.bfloat16)


def message_rows(sources, own_experts):
    per = sources * CAP
    base = per // 16 * 16
    left = per - base
    left_rows = -(-(own_experts * left) // 16) * 16
    total = own_experts * base + left_rows
    expert = np.zeros(total, np.int32)
    place = np.zeros(total, np.int32)
    valid = np.zeros(total, bool)
    for r in range(total):
        if r < own_experts * base:
            expert[r], place[r], valid[r] = r // base, r % base, True
        elif left and r - own_experts * base < own_experts * left:
            o = r - own_experts * base
            expert[r], place[r], valid[r] = o // left, base + o % left, True
    return base, left, left_rows, total, expert, place // CAP, place % CAP, valid


def moe_kernel(
    sizes,
    hn_ref,
    h1_ref,
    pick_ref,
    place_ref,
    chosen_ref,
    column_expert_ref,
    router_ref,
    gate_hbm,
    up_hbm,
    down_hbm,
    out_ref,
    hall,
    xs,
    xr,
    gate_buf,
    up_buf,
    down_buf,
    acc_g,
    acc_u,
    act,
    yr,
    left_acc,
    ps,
    pr,
    own_part,
    combine,
    wsem,
    hs_sem,
    hr_sem,
    xs_sem,
    xr_sem,
    ys_sem,
    yr_sem,
    ps_sem,
    pr_sem,
):
    nctx, nexp, epd, tok, base, left, left_rows, rm, chunks, cw = sizes
    my_c = lax.axis_index("ctx")
    my_e = lax.axis_index("exp")
    main = epd * base

    def exp_peer(d):
        return lax.rem(my_e + d, nexp)

    def ctx_peer(d):
        return lax.rem(my_c + d, nctx)

    def to_exp(src, dst, ss, rs, peer):
        return pltpu.make_async_remote_copy(
            src_ref=src, dst_ref=dst, send_sem=ss, recv_sem=rs,
            device_id=(my_c, peer), device_id_type=pl.DeviceIdType.MESH,
        )

    def to_ctx(src, dst, ss, rs, peer):
        return pltpu.make_async_remote_copy(
            src_ref=src, dst_ref=dst, send_sem=ss, recv_sem=rs,
            device_id=(peer, my_e), device_id_type=pl.DeviceIdType.MESH,
        )

    def weight_copies(k, slot):
        rows = pl.ds(pl.multiple_of(k * cw, cw), cw)
        return (
            pltpu.make_async_copy(gate_hbm.at[:, rows, :], gate_buf.at[slot], wsem.at[0, slot]),
            pltpu.make_async_copy(up_hbm.at[:, rows, :], up_buf.at[slot], wsem.at[1, slot]),
        )

    def down_copy(k, slot):
        columns = pl.ds(pl.multiple_of(k * cw, cw), cw)
        return pltpu.make_async_copy(
            down_hbm.at[:, :, columns], down_buf.at[slot], wsem.at[2, slot]
        )

    barrier = pltpu.get_barrier_semaphore()
    for d in range(1, nexp):
        pl.semaphore_signal(
            barrier, inc=1, device_id=(my_c, exp_peer(d)), device_id_type=pl.DeviceIdType.MESH
        )
    for d in range(1, nctx):
        pl.semaphore_signal(
            barrier, inc=1, device_id=(ctx_peer(d), my_e), device_id_type=pl.DeviceIdType.MESH
        )
    for k in range(2):
        for copy in weight_copies(k, k):
            copy.start()
        down_copy(k, k).start()
    pl.semaphore_wait(barrier, nexp - 1 + nctx - 1)

    def send_state(k):
        columns = pl.ds(pl.multiple_of(k * cw, cw), cw)

        def one(d, carry):
            to_exp(
                hn_ref.at[:, columns], hall.at[k, my_e], hs_sem.at[k, d], hr_sem.at[k, my_e],
                exp_peer(d),
            ).start()
            return carry

        lax.fori_loop(1, nexp, one, 0)
        hall[k, my_e] = hn_ref[:, columns]

    def loop(count, body):
        def step(k, carry):
            body(k)
            return carry

        lax.fori_loop(0, count, step, 0)

    loop(chunks, send_state)

    def dispatch(k):
        def arrived(d, carry):
            p = exp_peer(d)
            to_exp(
                hall.at[k, p], hall.at[k, p], hs_sem.at[k, d], hr_sem.at[k, p], p
            ).wait_recv()
            return carry

        lax.fori_loop(1, nexp, arrived, 0)
        states = hall[k].reshape(nexp * tok, cw)

        def rows_of(c):
            rows = pl.ds(pl.multiple_of(c * rm, 16), rm)
            return jnp.dot(
                pick_ref[rows, :], states, preferred_element_type=jnp.float32
            ).astype(jnp.bfloat16)

        def one(d, carry):
            c = ctx_peer(d)
            xs[k, c] = rows_of(c)
            to_ctx(xs.at[k, c], xr.at[k, my_c], xs_sem.at[k, d], xr_sem.at[k, my_c], c).start()
            return carry

        lax.fori_loop(1, nctx, one, 0)
        xr[k, my_c] = rows_of(my_c)

    loop(chunks, dispatch)

    logits = jnp.zeros((nexp * tok, router_ref.shape[1]), jnp.float32)
    for k in range(chunks):
        logits += jnp.dot(
            hall[k].reshape(nexp * tok, cw),
            router_ref[k * cw : (k + 1) * cw, :],
            preferred_element_type=jnp.float32,
        )
    raised = jnp.where(chosen_ref[...] > 0.5, jnp.exp(logits), 0.0)
    route_w = (raised / jnp.sum(raised, axis=-1, keepdims=True)).astype(jnp.bfloat16)
    combine[...] = (
        jnp.dot(route_w, column_expert_ref[...], preferred_element_type=jnp.float32).astype(
            jnp.bfloat16
        )
        * place_ref[...]
    )
    acc_g[...] = jnp.zeros_like(acc_g)
    acc_u[...] = jnp.zeros_like(acc_u)

    def enter(k):
        slot = lax.rem(k, 2)

        def arrived(d, carry):
            c = ctx_peer(d)
            to_ctx(xr.at[k, c], xr.at[k, c], xs_sem.at[k, d], xr_sem.at[k, c], c).wait_recv()
            return carry

        lax.fori_loop(1, nctx, arrived, 0)
        for copy in weight_copies(k, slot):
            copy.wait()

        def one(j, carry):
            front = xr[k, :, pl.ds(pl.multiple_of(j * base, 16), base), :].reshape(nctx * base, cw)
            gate_w, up_w = gate_buf[slot, j], up_buf[slot, j]
            top = pl.ds(0, nctx * base)
            acc_g[j, top, :] += jnp.dot(front, gate_w, preferred_element_type=jnp.float32)
            acc_u[j, top, :] += jnp.dot(front, up_w, preferred_element_type=jnp.float32)
            if left_rows:
                back = xr[k, :, main:rm, :].reshape(nctx * left_rows, cw)
                low = pl.ds(nctx * base, nctx * left_rows)
                acc_g[j, low, :] += jnp.dot(back, gate_w, preferred_element_type=jnp.float32)
                acc_u[j, low, :] += jnp.dot(back, up_w, preferred_element_type=jnp.float32)
            return carry

        lax.fori_loop(0, epd, one, 0)

        @pl.when(k + 2 < chunks)
        def _():
            for copy in weight_copies(k + 2, slot):
                copy.start()

    loop(chunks, enter)

    def activate(j):
        g = acc_g[j]
        act[j] = (g / (1.0 + jnp.exp(-g)) * acc_u[j]).astype(jnp.bfloat16)

    loop(epd, activate)

    def sent_states(k):
        def one(d, carry):
            p = exp_peer(d)
            to_exp(
                hn_ref.at[:, pl.ds(0, cw)], hall.at[k, my_e], hs_sem.at[k, d], hr_sem.at[k, my_e], p
            ).wait_send()
            return carry

        lax.fori_loop(1, nexp, one, 0)

        def two(d, carry):
            c = ctx_peer(d)
            to_ctx(
                xs.at[k, c], xr.at[k, my_c], xs_sem.at[k, d], xr_sem.at[k, my_c], c
            ).wait_send()
            return carry

        lax.fori_loop(1, nctx, two, 0)

    loop(chunks, sent_states)

    def leave(k):
        slot = lax.rem(k, 2)
        down_copy(k, slot).wait()
        if left_rows:
            left_acc[...] = jnp.zeros_like(left_acc)

        def one(j, carry):
            down_w = down_buf[slot, j]
            y = jnp.dot(act[j, : nctx * base, :], down_w, preferred_element_type=jnp.float32)
            xs[k, :, pl.ds(pl.multiple_of(j * base, 16), base), :] = y.astype(
                jnp.bfloat16
            ).reshape(nctx, base, cw)
            if left_rows:
                y2 = jnp.dot(act[j, nctx * base :, :], down_w, preferred_element_type=jnp.float32)
                row = lax.broadcasted_iota(jnp.int32, y2.shape, 0) % left_rows
                mine = (row >= j * left) & (row < (j + 1) * left)
                left_acc[...] += jnp.where(mine, y2, 0.0)
            return carry

        lax.fori_loop(0, epd, one, 0)
        if left_rows:
            xs[k, :, main:rm, :] = (
                left_acc[...].astype(jnp.bfloat16).reshape(nctx, left_rows, cw)
            )

        @pl.when(k + 2 < chunks)
        def _():
            down_copy(k + 2, slot).start()

        def push(d, carry):
            c = ctx_peer(d)
            to_ctx(xs.at[k, c], yr.at[k, my_c], ys_sem.at[k, d], yr_sem.at[k, my_c], c).start()
            return carry

        lax.fori_loop(1, nctx, push, 0)
        yr[k, my_c] = xs[k, my_c]

    loop(chunks, leave)

    def gather_back(k):
        def arrived(d, carry):
            c = ctx_peer(d)
            to_ctx(yr.at[k, c], yr.at[k, c], ys_sem.at[k, d], yr_sem.at[k, c], c).wait_recv()
            return carry

        lax.fori_loop(1, nctx, arrived, 0)
        back = yr[k].reshape(nctx * rm, cw)

        def part_of(s):
            rows = pl.ds(pl.multiple_of(s * tok, tok), tok)
            return jnp.dot(combine[rows, :], back, preferred_element_type=jnp.float32)

        def one(d, carry):
            s = exp_peer(d)
            ps[k, s] = part_of(s).astype(jnp.bfloat16)
            to_exp(ps.at[k, s], pr.at[k, my_e], ps_sem.at[k, d], pr_sem.at[k, my_e], s).start()
            return carry

        lax.fori_loop(1, nexp, one, 0)
        own_part[k] = part_of(my_e)

    loop(chunks, gather_back)

    def finish(k):
        columns = pl.ds(pl.multiple_of(k * cw, cw), cw)
        total = h1_ref[:, columns].astype(jnp.float32) + own_part[k]

        def one(d, total):
            p = exp_peer(d)
            to_exp(pr.at[k, p], pr.at[k, p], ps_sem.at[k, d], pr_sem.at[k, p], p).wait_recv()
            return total + pr[k, p].astype(jnp.float32)

        for d in range(1, nexp):
            total = one(d, total)
        out_ref[:, columns] = total.astype(jnp.bfloat16)

    loop(chunks, finish)

    def sent_back(k):
        def one(d, carry):
            s = exp_peer(d)
            to_exp(
                ps.at[k, s], pr.at[k, my_e], ps_sem.at[k, d], pr_sem.at[k, my_e], s
            ).wait_send()
            return carry

        lax.fori_loop(1, nexp, one, 0)

        def two(d, carry):
            c = ctx_peer(d)
            to_ctx(
                xs.at[k, c], yr.at[k, my_c], ys_sem.at[k, d], yr_sem.at[k, my_c], c
            ).wait_send()
            return carry

        lax.fori_loop(1, nctx, two, 0)

    loop(chunks, sent_back)


def expert_part(hn, h1, expert_ids, w_router, w_gate, w_up, w_down):
    nctx, nexp = lax.axis_size("ctx"), lax.axis_size("exp")
    my_e = lax.axis_index("exp")
    tok, width = hn.shape
    experts_all = w_router.shape[1]
    epd, _, hidden_units = w_gate.shape
    base, left, left_rows, rm, row_expert, row_source, row_slot, row_valid = message_rows(nexp, epd)
    rows_all = nctx * rm
    ids = lax.all_gather(expert_ids, "exp", axis=0, tiled=False)
    chosen = jnp.any(
        ids[:, :, :, None] == jnp.arange(experts_all, dtype=jnp.int32), axis=2
    )
    earlier = jnp.asarray(np.tril(np.ones((tok, tok), np.float32), -1), jnp.bfloat16)
    rank = jnp.einsum(
        "ut,ste->sue", earlier, chosen.astype(jnp.bfloat16), preferred_element_type=jnp.float32
    )
    code = jnp.where(chosen, rank, -1.0).reshape(nexp * tok, experts_all).astype(jnp.bfloat16)
    row_expert, row_source = np.tile(row_expert, nctx), np.tile(row_source, nctx)
    row_slot, row_valid = np.tile(row_slot, nctx), np.tile(row_valid, nctx)
    row_ctx = np.repeat(np.arange(nctx), rm)
    column_expert_id = jnp.asarray(row_ctx * nexp * epd + row_expert, jnp.int32) + my_e * epd
    column_expert = (
        jnp.arange(experts_all, dtype=jnp.int32)[:, None] == column_expert_id[None, :]
    ).astype(jnp.bfloat16)
    code_at = jnp.dot(code, column_expert, preferred_element_type=jnp.float32)
    token_source = np.arange(nexp * tok) // tok
    place = (
        (code_at == jnp.asarray(row_slot, jnp.float32)[None, :])
        & (jnp.asarray(token_source)[:, None] == jnp.asarray(row_source)[None, :])
        & jnp.asarray(row_valid)[None, :]
    ).astype(jnp.bfloat16)
    pick = place.T
    chunks = 4
    cw = width // chunks
    sizes = (nctx, nexp, epd, tok, base, left, left_rows, rm, chunks, cw)
    mr = nctx * (base + left_rows)
    bf = jnp.bfloat16
    vmem = pl.BlockSpec(memory_space=pltpu.VMEM)
    hbm = pl.BlockSpec(memory_space=pl.ANY)
    dma = pltpu.SemaphoreType.DMA
    return pl.pallas_call(
        functools.partial(moe_kernel, sizes),
        out_shape=jax.ShapeDtypeStruct((tok, width), bf),
        in_specs=[vmem] * 7 + [hbm] * 3,
        out_specs=vmem,
        scratch_shapes=[
            pltpu.VMEM((chunks, nexp, tok, cw), bf),
            pltpu.VMEM((chunks, nctx, rm, cw), bf),
            pltpu.VMEM((chunks, nctx, rm, cw), bf),
            pltpu.VMEM((2, epd, cw, hidden_units), bf),
            pltpu.VMEM((2, epd, cw, hidden_units), bf),
            pltpu.VMEM((2, epd, hidden_units, cw), bf),
            pltpu.VMEM((epd, mr, hidden_units), jnp.float32),
            pltpu.VMEM((epd, mr, hidden_units), jnp.float32),
            pltpu.VMEM((epd, mr, hidden_units), bf),
            pltpu.VMEM((chunks, nctx, rm, cw), bf),
            pltpu.VMEM((nctx * max(left_rows, 16), cw), jnp.float32),
            pltpu.VMEM((chunks, nexp, tok, cw), bf),
            pltpu.VMEM((chunks, nexp, tok, cw), bf),
            pltpu.VMEM((chunks, tok, cw), jnp.float32),
            pltpu.VMEM((nexp * tok, rows_all), bf),
            dma((3, 2)),
            dma((chunks, nexp)),
            dma((chunks, nexp)),
            dma((chunks, nctx)),
            dma((chunks, nctx)),
            dma((chunks, nctx)),
            dma((chunks, nctx)),
            dma((chunks, nexp)),
            dma((chunks, nexp)),
        ],
        compiler_params=pltpu.CompilerParams(
            collective_id=0, has_side_effects=True, vmem_limit_bytes=63 * 1024 * 1024
        ),
        cost_estimate=pl.CostEstimate(
            flops=6 * epd * mr * width * hidden_units,
            bytes_accessed=6 * epd * width * hidden_units,
            transcendentals=0,
        ),
    )(
        hn,
        h1,
        pick,
        place,
        chosen.reshape(nexp * tok, experts_all).astype(jnp.float32),
        column_expert,
        w_router,
        w_gate,
        w_up,
        w_down,
    )


def local(
    hidden, queries, keys, values, w_out, norm_gain, w_router, expert_ids, w_gate, w_up, w_down
):
    tok_rows = hidden.shape[0]
    kv_heads = keys.shape[1] // DH
    q_heads = queries.shape[1] // DH
    group = q_heads // kv_heads
    device = lax.axis_index(("ctx", "exp"))
    first_row = device * tok_rows
    positions = first_row + jnp.arange(tok_rows, dtype=jnp.int32)
    cos_table, sin_table = yarn_tables(positions, DH)
    q_four = rotate(queries.reshape(tok_rows, q_heads, DH), cos_table, sin_table).reshape(
        tok_rows, kv_heads, group, DH
    )
    k_flat = rotate(keys.reshape(tok_rows, kv_heads, DH), cos_table, sin_table).reshape(
        tok_rows, kv_heads * DH
    )
    q_rows = first_row + jnp.arange(tok_rows, dtype=jnp.int32)
    scale = 1.0 / math.sqrt(DH)

    def update(carry, operands):
        run_max, run_sum, run_acc = carry
        key_block, value_block, block_start = operands
        block_len = key_block.shape[0]
        scores = (
            jnp.einsum("thgd,phd->thgp", q_four, key_block, preferred_element_type=jnp.float32)
            * scale
        )
        key_rows = block_start + jnp.arange(block_len, dtype=jnp.int32)
        allowed = (key_rows[None, :] <= q_rows[:, None])[:, None, None, :]
        scores = jnp.where(allowed, scores, -1e30)
        new_max = jnp.maximum(run_max, jnp.max(scores, axis=-1))
        weights = jnp.where(allowed, jnp.exp(scores - new_max[..., None]), 0.0)
        factor = jnp.exp(run_max - new_max)
        new_sum = run_sum * factor + jnp.sum(weights, axis=-1)
        added = jnp.einsum(
            "thgp,phd->thgd",
            weights.astype(jnp.bfloat16),
            value_block,
            preferred_element_type=jnp.float32,
        )
        return ((new_max, new_sum, run_acc * factor[..., None] + added), None)

    initial = (
        jnp.full((tok_rows, kv_heads, group), -1e30, jnp.float32),
        jnp.zeros((tok_rows, kv_heads, group), jnp.float32),
        jnp.zeros((tok_rows, kv_heads, group, DH), jnp.float32),
    )
    key_piece = lax.all_gather(k_flat, ("ctx", "exp"), axis=0, tiled=True)
    value_piece = lax.all_gather(values, ("ctx", "exp"), axis=0, tiled=True)
    piece_len = key_piece.shape[0]
    block_len = math.gcd(piece_len, 1024)
    count = piece_len // block_len
    key_blocks = key_piece.reshape(count, block_len, kv_heads, DH)
    value_blocks = value_piece.reshape(count, block_len, kv_heads, DH)
    offsets = jnp.arange(count, dtype=jnp.int32) * block_len
    result, unused = lax.scan(update, initial, (key_blocks, value_blocks, offsets))
    final_max, final_sum, final_acc = result
    attn = (final_acc / final_sum[..., None]).astype(jnp.bfloat16).reshape(tok_rows, q_heads * DH)
    h1 = (
        jnp.dot(attn, w_out, preferred_element_type=jnp.float32) + hidden.astype(jnp.float32)
    ).astype(jnp.bfloat16)
    h1_f = h1.astype(jnp.float32)
    normed = (
        h1_f / jnp.sqrt(jnp.mean(h1_f * h1_f, axis=-1, keepdims=True) + 1e-06) * norm_gain[None, :]
    )
    hn = normed.astype(jnp.bfloat16)
    mixed = expert_part(hn, h1, expert_ids, w_router, w_gate, w_up, w_down)
    return mixed


def solution(mesh):
    in_specs = (
        P(("ctx", "exp"), None),
        P(("ctx", "exp"), None),
        P(("ctx", "exp"), None),
        P(("ctx", "exp"), None),
        P(),
        P(),
        P(),
        P(("ctx", "exp"), None),
        P(("ctx", "exp"), None, None),
        P(("ctx", "exp"), None, None),
        P(("ctx", "exp"), None, None),
    )
    out_specs = P(("ctx", "exp"), None)
    return jax.shard_map(local, mesh=mesh, in_specs=in_specs, out_specs=out_specs, check_vma=False)
```

```python
import functools
import math

import jax
import jax.numpy as jnp
import numpy as np
from jax import lax
from jax.experimental import pallas as pl
from jax.experimental.pallas import tpu as pltpu
from jax.sharding import PartitionSpec as P

DH = 128
CAP = 9


rope_base = 1000000.0
yarn_factor = 4.0
orig_len = 32768.0
beta_fast = 32.0
beta_slow = 1.0
mscale_yarn = 0.1 * math.log(4.0) + 1.0


def yarn_tables(positions, head_size):
    half_size = head_size // 2
    index_f = jnp.arange(half_size, dtype=jnp.float32)
    pos_freq = rope_base ** (2.0 * index_f / head_size)
    inv_extra = 1.0 / pos_freq
    inv_inter = 1.0 / (yarn_factor * pos_freq)
    low_dim = max(
        math.floor(
            head_size
            * math.log(orig_len / (beta_fast * 2.0 * math.pi))
            / (2.0 * math.log(rope_base))
        ),
        0,
    )
    high_dim = min(
        math.ceil(
            head_size
            * math.log(orig_len / (beta_slow * 2.0 * math.pi))
            / (2.0 * math.log(rope_base))
        ),
        head_size - 1,
    )
    ramp_part = jnp.clip((index_f - low_dim) / max(high_dim - low_dim, 0.001), 0.0, 1.0)
    extra_part = 1.0 - ramp_part
    inverse = inv_inter * (1.0 - extra_part) + inv_extra * extra_part
    angles = positions.astype(jnp.float32)[:, None] * inverse[None, :]
    angles = jnp.concatenate([angles, angles], axis=-1)
    return (jnp.cos(angles) * mscale_yarn, jnp.sin(angles) * mscale_yarn)


def rotate(vectors, cos_table, sin_table):
    values_f = vectors.astype(jnp.float32)
    half_size = values_f.shape[-1] // 2
    turned = jnp.concatenate([-values_f[..., half_size:], values_f[..., :half_size]], axis=-1)
    return (values_f * cos_table[:, None, :] + turned * sin_table[:, None, :]).astype(jnp.bfloat16)


def message_rows(sources, own_experts):
    per = sources * CAP
    base = per // 16 * 16
    left = per - base
    left_rows = -(-(own_experts * left) // 16) * 16
    total = own_experts * base + left_rows
    expert = np.zeros(total, np.int32)
    place = np.zeros(total, np.int32)
    valid = np.zeros(total, bool)
    for r in range(total):
        if r < own_experts * base:
            expert[r], place[r], valid[r] = r // base, r % base, True
        elif left and r - own_experts * base < own_experts * left:
            o = r - own_experts * base
            expert[r], place[r], valid[r] = o // left, base + o % left, True
    return base, left, left_rows, total, expert, place // CAP, place % CAP, valid


def moe_kernel(
    sizes,
    hn_ref,
    h1_ref,
    pick_ref,
    place_ref,
    chosen_ref,
    column_expert_ref,
    router_ref,
    gate_hbm,
    up_hbm,
    down_hbm,
    out_ref,
    hall,
    xs,
    xr,
    gate_buf,
    up_buf,
    down_buf,
    acc_g,
    acc_u,
    act,
    yr,
    left_acc,
    ps,
    pr,
    own_part,
    combine,
    wsem,
    hs_sem,
    hr_sem,
    xs_sem,
    xr_sem,
    ys_sem,
    yr_sem,
    ps_sem,
    pr_sem,
):
    nctx, nexp, epd, tok, base, left, left_rows, rm, chunks, cw = sizes
    my_c = lax.axis_index("ctx")
    my_e = lax.axis_index("exp")
    main = epd * base

    def exp_peer(d):
        return lax.rem(my_e + d, nexp)

    def ctx_peer(d):
        return lax.rem(my_c + d, nctx)

    def to_exp(src, dst, ss, rs, peer):
        return pltpu.make_async_remote_copy(
            src_ref=src, dst_ref=dst, send_sem=ss, recv_sem=rs,
            device_id=(my_c, peer), device_id_type=pl.DeviceIdType.MESH,
        )

    def to_ctx(src, dst, ss, rs, peer):
        return pltpu.make_async_remote_copy(
            src_ref=src, dst_ref=dst, send_sem=ss, recv_sem=rs,
            device_id=(peer, my_e), device_id_type=pl.DeviceIdType.MESH,
        )

    def weight_copies(k, slot):
        rows = pl.ds(pl.multiple_of(k * cw, cw), cw)
        return (
            pltpu.make_async_copy(gate_hbm.at[:, rows, :], gate_buf.at[slot], wsem.at[0, slot]),
            pltpu.make_async_copy(up_hbm.at[:, rows, :], up_buf.at[slot], wsem.at[1, slot]),
        )

    def down_copy(k, slot):
        columns = pl.ds(pl.multiple_of(k * cw, cw), cw)
        return pltpu.make_async_copy(
            down_hbm.at[:, :, columns], down_buf.at[slot], wsem.at[2, slot]
        )

    barrier = pltpu.get_barrier_semaphore()
    for d in range(1, nexp):
        pl.semaphore_signal(
            barrier, inc=1, device_id=(my_c, exp_peer(d)), device_id_type=pl.DeviceIdType.MESH
        )
    for d in range(1, nctx):
        pl.semaphore_signal(
            barrier, inc=1, device_id=(ctx_peer(d), my_e), device_id_type=pl.DeviceIdType.MESH
        )
    for k in range(2):
        for copy in weight_copies(k, k):
            copy.start()
        down_copy(k, k).start()
    pl.semaphore_wait(barrier, nexp - 1 + nctx - 1)

    def send_state(k):
        columns = pl.ds(pl.multiple_of(k * cw, cw), cw)

        def one(d, carry):
            to_exp(
                hn_ref.at[:, columns], hall.at[k, my_e], hs_sem.at[k, d], hr_sem.at[k, my_e],
                exp_peer(d),
            ).start()
            return carry

        lax.fori_loop(1, nexp, one, 0)
        hall[k, my_e] = hn_ref[:, columns]

    def loop(count, body):
        def step(k, carry):
            body(k)
            return carry

        lax.fori_loop(0, count, step, 0)

    loop(chunks, send_state)

    def dispatch(k):
        def arrived(d, carry):
            p = exp_peer(d)
            to_exp(
                hall.at[k, p], hall.at[k, p], hs_sem.at[k, d], hr_sem.at[k, p], p
            ).wait_recv()
            return carry

        lax.fori_loop(1, nexp, arrived, 0)
        states = hall[k].reshape(nexp * tok, cw)

        def rows_of(c):
            rows = pl.ds(pl.multiple_of(c * rm, 16), rm)
            return jnp.dot(
                pick_ref[rows, :], states, preferred_element_type=jnp.float32
            ).astype(jnp.bfloat16)

        def one(d, carry):
            c = ctx_peer(d)
            xs[k, c] = rows_of(c)
            to_ctx(xs.at[k, c], xr.at[k, my_c], xs_sem.at[k, d], xr_sem.at[k, my_c], c).start()
            return carry

        lax.fori_loop(1, nctx, one, 0)
        xr[k, my_c] = rows_of(my_c)

    loop(chunks, dispatch)

    logits = jnp.zeros((nexp * tok, router_ref.shape[1]), jnp.float32)
    for k in range(chunks):
        logits += jnp.dot(
            hall[k].reshape(nexp * tok, cw),
            router_ref[k * cw : (k + 1) * cw, :],
            preferred_element_type=jnp.float32,
        )
    raised = jnp.where(chosen_ref[...] > 0.5, jnp.exp(logits), 0.0)
    route_w = (raised / jnp.sum(raised, axis=-1, keepdims=True)).astype(jnp.bfloat16)
    combine[...] = (
        jnp.dot(route_w, column_expert_ref[...], preferred_element_type=jnp.float32).astype(
            jnp.bfloat16
        )
        * place_ref[...]
    )
    acc_g[...] = jnp.zeros_like(acc_g)
    acc_u[...] = jnp.zeros_like(acc_u)

    def enter(k):
        slot = lax.rem(k, 2)

        def arrived(d, carry):
            c = ctx_peer(d)
            to_ctx(xr.at[k, c], xr.at[k, c], xs_sem.at[k, d], xr_sem.at[k, c], c).wait_recv()
            return carry

        lax.fori_loop(1, nctx, arrived, 0)
        for copy in weight_copies(k, slot):
            copy.wait()

        def one(j, carry):
            front = xr[k, :, pl.ds(pl.multiple_of(j * base, 16), base), :].reshape(nctx * base, cw)
            gate_w, up_w = gate_buf[slot, j], up_buf[slot, j]
            top = pl.ds(0, nctx * base)
            acc_g[j, top, :] += jnp.dot(front, gate_w, preferred_element_type=jnp.float32)
            acc_u[j, top, :] += jnp.dot(front, up_w, preferred_element_type=jnp.float32)
            if left_rows:
                back = xr[k, :, main:rm, :].reshape(nctx * left_rows, cw)
                low = pl.ds(nctx * base, nctx * left_rows)
                acc_g[j, low, :] += jnp.dot(back, gate_w, preferred_element_type=jnp.float32)
                acc_u[j, low, :] += jnp.dot(back, up_w, preferred_element_type=jnp.float32)
            return carry

        lax.fori_loop(0, epd, one, 0)

        @pl.when(k + 2 < chunks)
        def _():
            for copy in weight_copies(k + 2, slot):
                copy.start()

    loop(chunks, enter)

    def activate(j):
        g = acc_g[j]
        act[j] = (g / (1.0 + jnp.exp(-g)) * acc_u[j]).astype(jnp.bfloat16)

    loop(epd, activate)

    def sent_states(k):
        def one(d, carry):
            p = exp_peer(d)
            to_exp(
                hn_ref.at[:, pl.ds(0, cw)], hall.at[k, my_e], hs_sem.at[k, d], hr_sem.at[k, my_e], p
            ).wait_send()
            return carry

        lax.fori_loop(1, nexp, one, 0)

        def two(d, carry):
            c = ctx_peer(d)
            to_ctx(
                xs.at[k, c], xr.at[k, my_c], xs_sem.at[k, d], xr_sem.at[k, my_c], c
            ).wait_send()
            return carry

        lax.fori_loop(1, nctx, two, 0)

    loop(chunks, sent_states)

    def leave(k):
        slot = lax.rem(k, 2)
        down_copy(k, slot).wait()
        if left_rows:
            left_acc[...] = jnp.zeros_like(left_acc)

        def one(j, carry):
            down_w = down_buf[slot, j]
            y = jnp.dot(act[j, : nctx * base, :], down_w, preferred_element_type=jnp.float32)
            xs[k, :, pl.ds(pl.multiple_of(j * base, 16), base), :] = y.astype(
                jnp.bfloat16
            ).reshape(nctx, base, cw)
            if left_rows:
                y2 = jnp.dot(act[j, nctx * base :, :], down_w, preferred_element_type=jnp.float32)
                row = lax.broadcasted_iota(jnp.int32, y2.shape, 0) % left_rows
                mine = (row >= j * left) & (row < (j + 1) * left)
                left_acc[...] += jnp.where(mine, y2, 0.0)
            return carry

        lax.fori_loop(0, epd, one, 0)
        if left_rows:
            xs[k, :, main:rm, :] = (
                left_acc[...].astype(jnp.bfloat16).reshape(nctx, left_rows, cw)
            )

        @pl.when(k + 2 < chunks)
        def _():
            down_copy(k + 2, slot).start()

        def push(d, carry):
            c = ctx_peer(d)
            to_ctx(xs.at[k, c], yr.at[k, my_c], ys_sem.at[k, d], yr_sem.at[k, my_c], c).start()
            return carry

        lax.fori_loop(1, nctx, push, 0)
        yr[k, my_c] = xs[k, my_c]

    loop(chunks, leave)

    def gather_back(k):
        def arrived(d, carry):
            c = ctx_peer(d)
            to_ctx(yr.at[k, c], yr.at[k, c], ys_sem.at[k, d], yr_sem.at[k, c], c).wait_recv()
            return carry

        lax.fori_loop(1, nctx, arrived, 0)
        back = yr[k].reshape(nctx * rm, cw)

        def part_of(s):
            rows = pl.ds(pl.multiple_of(s * tok, tok), tok)
            return jnp.dot(combine[rows, :], back, preferred_element_type=jnp.float32)

        def one(d, carry):
            s = exp_peer(d)
            ps[k, s] = part_of(s).astype(jnp.bfloat16)
            to_exp(ps.at[k, s], pr.at[k, my_e], ps_sem.at[k, d], pr_sem.at[k, my_e], s).start()
            return carry

        lax.fori_loop(1, nexp, one, 0)
        own_part[k] = part_of(my_e)

    loop(chunks, gather_back)

    def finish(k):
        columns = pl.ds(pl.multiple_of(k * cw, cw), cw)
        total = h1_ref[:, columns].astype(jnp.float32) + own_part[k]

        def one(d, total):
            p = exp_peer(d)
            to_exp(pr.at[k, p], pr.at[k, p], ps_sem.at[k, d], pr_sem.at[k, p], p).wait_recv()
            return total + pr[k, p].astype(jnp.float32)

        for d in range(1, nexp):
            total = one(d, total)
        out_ref[:, columns] = total.astype(jnp.bfloat16)

    loop(chunks, finish)

    def sent_back(k):
        def one(d, carry):
            s = exp_peer(d)
            to_exp(
                ps.at[k, s], pr.at[k, my_e], ps_sem.at[k, d], pr_sem.at[k, my_e], s
            ).wait_send()
            return carry

        lax.fori_loop(1, nexp, one, 0)

        def two(d, carry):
            c = ctx_peer(d)
            to_ctx(
                xs.at[k, c], yr.at[k, my_c], ys_sem.at[k, d], yr_sem.at[k, my_c], c
            ).wait_send()
            return carry

        lax.fori_loop(1, nctx, two, 0)

    loop(chunks, sent_back)


def expert_part(hn, h1, ids, w_router, w_gate, w_up, w_down):
    nctx, nexp = lax.axis_size("ctx"), lax.axis_size("exp")
    my_e = lax.axis_index("exp")
    tok, width = hn.shape
    experts_all = w_router.shape[1]
    epd, _, hidden_units = w_gate.shape
    base, left, left_rows, rm, row_expert, row_source, row_slot, row_valid = message_rows(nexp, epd)
    rows_all = nctx * rm
    chosen = jnp.any(
        ids[:, :, :, None] == jnp.arange(experts_all, dtype=jnp.int32), axis=2
    )
    earlier = jnp.asarray(np.tril(np.ones((tok, tok), np.float32), -1), jnp.bfloat16)
    rank = jnp.einsum(
        "ut,ste->sue", earlier, chosen.astype(jnp.bfloat16), preferred_element_type=jnp.float32
    )
    code = jnp.where(chosen, rank, -1.0).reshape(nexp * tok, experts_all).astype(jnp.bfloat16)
    row_expert, row_source = np.tile(row_expert, nctx), np.tile(row_source, nctx)
    row_slot, row_valid = np.tile(row_slot, nctx), np.tile(row_valid, nctx)
    row_ctx = np.repeat(np.arange(nctx), rm)
    column_expert_id = jnp.asarray(row_ctx * nexp * epd + row_expert, jnp.int32) + my_e * epd
    column_expert = (
        jnp.arange(experts_all, dtype=jnp.int32)[:, None] == column_expert_id[None, :]
    ).astype(jnp.bfloat16)
    code_at = jnp.dot(code, column_expert, preferred_element_type=jnp.float32)
    token_source = np.arange(nexp * tok) // tok
    place = (
        (code_at == jnp.asarray(row_slot, jnp.float32)[None, :])
        & (jnp.asarray(token_source)[:, None] == jnp.asarray(row_source)[None, :])
        & jnp.asarray(row_valid)[None, :]
    ).astype(jnp.bfloat16)
    pick = place.T
    chunks = 4
    cw = width // chunks
    sizes = (nctx, nexp, epd, tok, base, left, left_rows, rm, chunks, cw)
    mr = nctx * (base + left_rows)
    bf = jnp.bfloat16
    vmem = pl.BlockSpec(memory_space=pltpu.VMEM)
    hbm = pl.BlockSpec(memory_space=pl.ANY)
    dma = pltpu.SemaphoreType.DMA
    return pl.pallas_call(
        functools.partial(moe_kernel, sizes),
        out_shape=jax.ShapeDtypeStruct((tok, width), bf),
        in_specs=[vmem] * 7 + [hbm] * 3,
        out_specs=vmem,
        scratch_shapes=[
            pltpu.VMEM((chunks, nexp, tok, cw), bf),
            pltpu.VMEM((chunks, nctx, rm, cw), bf),
            pltpu.VMEM((chunks, nctx, rm, cw), bf),
            pltpu.VMEM((2, epd, cw, hidden_units), bf),
            pltpu.VMEM((2, epd, cw, hidden_units), bf),
            pltpu.VMEM((2, epd, hidden_units, cw), bf),
            pltpu.VMEM((epd, mr, hidden_units), jnp.float32),
            pltpu.VMEM((epd, mr, hidden_units), jnp.float32),
            pltpu.VMEM((epd, mr, hidden_units), bf),
            pltpu.VMEM((chunks, nctx, rm, cw), bf),
            pltpu.VMEM((nctx * max(left_rows, 16), cw), jnp.float32),
            pltpu.VMEM((chunks, nexp, tok, cw), bf),
            pltpu.VMEM((chunks, nexp, tok, cw), bf),
            pltpu.VMEM((chunks, tok, cw), jnp.float32),
            pltpu.VMEM((nexp * tok, rows_all), bf),
            dma((3, 2)),
            dma((chunks, nexp)),
            dma((chunks, nexp)),
            dma((chunks, nctx)),
            dma((chunks, nctx)),
            dma((chunks, nctx)),
            dma((chunks, nctx)),
            dma((chunks, nexp)),
            dma((chunks, nexp)),
        ],
        compiler_params=pltpu.CompilerParams(
            collective_id=0, has_side_effects=True, vmem_limit_bytes=63 * 1024 * 1024
        ),
        cost_estimate=pl.CostEstimate(
            flops=6 * epd * mr * width * hidden_units,
            bytes_accessed=6 * epd * width * hidden_units,
            transcendentals=0,
        ),
    )(
        hn,
        h1,
        pick,
        place,
        chosen.reshape(nexp * tok, experts_all).astype(jnp.float32),
        column_expert,
        w_router,
        w_gate,
        w_up,
        w_down,
    )


def attend_kernel(
    sizes,
    q_ref,
    kv_ref,
    ids_ref,
    out_ref,
    ids_out,
    kv,
    ids_all,
    peak,
    total,
    acc,
    is_sem,
    ir_sem,
    zs_sem,
    zr_sem,
    xs_sem,
    xr_sem,
    fs_sem,
    fr_sem,
):
    nctx, nexp, tok, kv_heads, group = sizes
    my_c, my_e = lax.axis_index("ctx"), lax.axis_index("exp")
    pairs = nctx // 2
    my_h, core = my_c // 2, lax.rem(my_c, 2)
    partner = my_h * 2 + 1 - core
    mesh_id = pl.DeviceIdType.MESH

    def exp_peer(d):
        return lax.rem(my_e + d, nexp)

    def pair_peer(d):
        return lax.rem(my_h + d, pairs)

    def copy_to(src, dst, ss, rs, c, e):
        return pltpu.make_async_remote_copy(
            src_ref=src, dst_ref=dst, send_sem=ss, recv_sem=rs,
            device_id=(c, e), device_id_type=mesh_id,
        )

    def to_exp(d):
        return copy_to(
            kv_ref, kv.at[my_c, my_e], zs_sem.at[d], zr_sem.at[my_e], my_c, exp_peer(d)
        )

    def ids_to(d):
        return copy_to(
            ids_ref, ids_all.at[my_e], is_sem.at[d], ir_sem.at[my_e], my_c, exp_peer(d)
        )

    def to_pair(s, d):
        return copy_to(
            kv.at[my_c, s], kv.at[my_c, s], xs_sem.at[s, d], xr_sem.at[s, my_h],
            pair_peer(d) * 2 + core, my_e,
        )

    def to_partner(s, h):
        c = h * 2 + core
        return copy_to(
            kv.at[c, s], kv.at[c, s], fs_sem.at[s, h], fr_sem.at[s, h], partner, my_e
        )

    barrier = pltpu.get_barrier_semaphore()
    for d in range(1, nexp):
        pl.semaphore_signal(
            barrier, inc=1, device_id=(my_c, exp_peer(d)), device_id_type=mesh_id
        )
    for d in range(1, pairs):
        pl.semaphore_signal(
            barrier, inc=1, device_id=(pair_peer(d) * 2 + core, my_e), device_id_type=mesh_id
        )
    pl.semaphore_signal(barrier, inc=1, device_id=(partner, my_e), device_id_type=mesh_id)
    kv[my_c, my_e] = kv_ref[...]
    ids_all[my_e] = ids_ref[...]
    pl.semaphore_wait(barrier, nexp - 1 + pairs - 1 + 1)

    def loop(low, high, body):
        def step(i, carry):
            body(i)
            return carry

        lax.fori_loop(low, high, step, 0)

    loop(1, nexp, lambda d: to_exp(d).start())
    loop(1, nexp, lambda d: ids_to(d).start())

    def spread(s):
        loop(1, pairs, lambda d: to_pair(s, d).start())
        to_partner(s, my_h).start()

    spread(my_e)

    def from_exp(d):
        s = exp_peer(d)
        copy_to(
            kv.at[my_c, s], kv.at[my_c, s], zs_sem.at[d], zr_sem.at[s], my_c, s
        ).wait_recv()
        spread(s)

    loop(1, nexp, from_exp)

    factor = (1.0 / math.sqrt(DH)) * math.log2(math.e)
    span = nexp * tok
    heads = 2 if group % 2 == 0 else 1
    rows = heads * tok

    def block(c, first):
        def one(i, carry):
            at = pl.ds(pl.multiple_of(i * rows, rows), rows)
            q = q_ref[at, :]
            g = i * heads // group
            head_cols = pl.ds(pl.multiple_of(g * DH, DH), DH)
            value_cols = pl.ds(pl.multiple_of((kv_heads + g) * DH, DH), DH)
            k = kv[c, :, :, head_cols].reshape(span, DH)
            v = kv[c, :, :, value_cols].reshape(span, DH)
            scores = lax.dot_general(
                q, k, (((1,), (1,)), ((), ())), preferred_element_type=jnp.float32
            ) * factor
            if first:
                t = lax.broadcasted_iota(jnp.int32, scores.shape, 0) % tok
                u = lax.broadcasted_iota(jnp.int32, scores.shape, 1)
                scores = jnp.where(u <= t + my_e * tok, scores, -1e30)
                top = jnp.max(scores, axis=-1, keepdims=True)
                w = jnp.exp2(scores - top)
                total[at, :] = jnp.broadcast_to(jnp.sum(w, axis=-1, keepdims=True), (rows, DH))
                peak[at, :] = jnp.broadcast_to(top, (rows, DH))
                acc[at, :] = jnp.dot(
                    w.astype(jnp.bfloat16), v, preferred_element_type=jnp.float32
                )
            else:
                old = peak[at, :]
                new = jnp.maximum(old, jnp.max(scores, axis=-1, keepdims=True))
                w = jnp.exp2(scores - new[:, :1])
                fade = jnp.exp2(old - new)
                total[at, :] = total[at, :] * fade + jnp.sum(w, axis=-1, keepdims=True)
                peak[at, :] = new
                acc[at, :] = acc[at, :] * fade + jnp.dot(
                    w.astype(jnp.bfloat16), v, preferred_element_type=jnp.float32
                )
            return carry

        lax.fori_loop(0, kv_heads * group // heads, one, 0)

    block(my_c, True)

    def forward(s):
        def one(d):
            h = pair_peer(d)
            c = h * 2 + core
            copy_to(
                kv.at[c, s], kv.at[c, s], xs_sem.at[s, d], xr_sem.at[s, h], c, my_e
            ).wait_recv()
            to_partner(s, h).start()

        loop(1, pairs, one)

    loop(0, nexp, forward)

    def same_core(d):
        c = pair_peer(d) * 2 + core

        @pl.when(c < my_c)
        def _():
            block(c, False)

    loop(1, pairs, same_core)

    def other_core(d):
        h = pair_peer(d)
        c = h * 2 + 1 - core

        def arrived(s):
            copy_to(
                kv.at[c, s], kv.at[c, s], fs_sem.at[s, h], fr_sem.at[s, h], partner, my_e
            ).wait_recv()

        loop(0, nexp, arrived)

        @pl.when(c < my_c)
        def _():
            block(c, False)

    loop(0, pairs, other_core)

    for i in range(kv_heads * group):
        at = slice(i * tok, (i + 1) * tok)
        out_ref[:, i * DH : (i + 1) * DH] = (acc[at, :] / total[at, :]).astype(jnp.bfloat16)

    def from_ids(d):
        s = exp_peer(d)
        copy_to(
            ids_all.at[s], ids_all.at[s], is_sem.at[d], ir_sem.at[s], my_c, s
        ).wait_recv()

    loop(1, nexp, from_ids)
    ids_out[...] = ids_all[...]

    def sent(s):
        loop(1, pairs, lambda d: to_pair(s, d).wait_send())
        loop(0, pairs, lambda h: to_partner(s, h).wait_send())

    loop(0, nexp, sent)
    loop(1, nexp, lambda d: to_exp(d).wait_send())
    loop(1, nexp, lambda d: ids_to(d).wait_send())


def attend(q, kv, expert_ids, kv_heads, group):
    nctx, nexp = lax.axis_size("ctx"), lax.axis_size("exp")
    tok, width = kv.shape
    bf = jnp.bfloat16
    rows = q.shape[0]
    vmem = pl.BlockSpec(memory_space=pltpu.VMEM)
    dma = pltpu.SemaphoreType.DMA
    return pl.pallas_call(
        functools.partial(attend_kernel, (nctx, nexp, tok, kv_heads, group)),
        out_shape=(
            jax.ShapeDtypeStruct((tok, kv_heads * group * DH), bf),
            jax.ShapeDtypeStruct((nexp,) + expert_ids.shape, jnp.int32),
        ),
        in_specs=[vmem] * 3,
        out_specs=(vmem, vmem),
        scratch_shapes=[
            pltpu.VMEM((nctx, nexp, tok, width), bf),
            pltpu.VMEM((nexp,) + expert_ids.shape, jnp.int32),
            pltpu.VMEM((rows, DH), jnp.float32),
            pltpu.VMEM((rows, DH), jnp.float32),
            pltpu.VMEM((rows, DH), jnp.float32),
            dma((nexp,)),
            dma((nexp,)),
            dma((nexp,)),
            dma((nexp,)),
            dma((nexp, nctx // 2)),
            dma((nexp, nctx // 2)),
            dma((nexp, nctx // 2)),
            dma((nexp, nctx // 2)),
        ],
        compiler_params=pltpu.CompilerParams(
            collective_id=1, has_side_effects=True, vmem_limit_bytes=48 * 1024 * 1024
        ),
        cost_estimate=pl.CostEstimate(
            flops=4 * rows * nctx * nexp * tok * DH,
            bytes_accessed=nctx * nexp * tok * width * 2,
            transcendentals=rows * nctx * nexp * tok,
        ),
    )(q, kv, expert_ids)


def local(
    hidden, queries, keys, values, w_out, norm_gain, w_router, expert_ids, w_gate, w_up, w_down
):
    tok_rows = hidden.shape[0]
    kv_heads = keys.shape[1] // DH
    q_heads = queries.shape[1] // DH
    group = q_heads // kv_heads
    device = lax.axis_index(("ctx", "exp"))
    first_row = device * tok_rows
    positions = first_row + jnp.arange(tok_rows, dtype=jnp.int32)
    cos_table, sin_table = yarn_tables(positions, DH)
    q_rows = jnp.swapaxes(
        rotate(queries.reshape(tok_rows, q_heads, DH), cos_table, sin_table), 0, 1
    ).reshape(q_heads * tok_rows, DH)
    k_flat = rotate(keys.reshape(tok_rows, kv_heads, DH), cos_table, sin_table).reshape(
        tok_rows, kv_heads * DH
    )
    attn, ids = attend(
        q_rows, jnp.concatenate([k_flat, values], axis=1), expert_ids, kv_heads, group
    )
    h1 = (
        jnp.dot(attn, w_out, preferred_element_type=jnp.float32) + hidden.astype(jnp.float32)
    ).astype(jnp.bfloat16)
    h1_f = h1.astype(jnp.float32)
    normed = (
        h1_f / jnp.sqrt(jnp.mean(h1_f * h1_f, axis=-1, keepdims=True) + 1e-06) * norm_gain[None, :]
    )
    hn = normed.astype(jnp.bfloat16)
    mixed = expert_part(hn, h1, ids, w_router, w_gate, w_up, w_down)
    return mixed


def solution(mesh):
    in_specs = (
        P(("ctx", "exp"), None),
        P(("ctx", "exp"), None),
        P(("ctx", "exp"), None),
        P(("ctx", "exp"), None),
        P(),
        P(),
        P(),
        P(("ctx", "exp"), None),
        P(("ctx", "exp"), None, None),
        P(("ctx", "exp"), None, None),
        P(("ctx", "exp"), None, None),
    )
    out_specs = P(("ctx", "exp"), None)
    return jax.shard_map(local, mesh=mesh, in_specs=in_specs, out_specs=out_specs, check_vma=False)
```
